128 devices in a mesh: row: 8 (over z_lo, x), col: 16 (over y, z_hi, core).
Axes of the slice: x: 4, y: 4, z: 4 (z_hi: 2, z_lo: 2; z = z_hi * 2 + z_lo), core: 2. Of those that a mesh axis runs over, the one named last changes fastest.
Arguments:
- anchor_features: float32 [16384, 1024], P(('row', 'col')), may hold values from -6 to 6
- candidate_features: float32 [16384, 1024], P(('row', 'col')), may hold values from -6 to 6
- anchor_sample_ids: int32 [16384], replicated, may hold values from 0 to 4095
- candidate_sample_ids: int32 [16384], replicated, may hold values from 0 to 4095
- opponent_tile: int32 [3, 128], replicated, may hold values from 0 to 127, as said below
- sharpness_array: float32 [1], replicated, may hold values from 8 to 16
- score_offset: float32 [1], replicated, may hold values from -3 to 0
Outputs:
- grad_a: float32 [16384, 1024], P(('row', 'col'))
- grad_b: float32 [16384, 1024], P(('row', 'col'))
The draws below stay inside these ranges and needn't reach their ends.
Inputs may be any that keep to these rules, and one draw needn't show every extreme that they name: Each row opponent_tile[k] is a perfect pairing of the blocks: opponent_tile[k, opponent_tile[k, q]] = q and opponent_tile[k, q] != q. The 3 rows are consecutive rounds of one round-robin tournament over relabelled blocks, so no two rounds pair the same blocks.
All inputs are finite; a program needn't handle non-finite values.
Results may differ from the reference program's by a relative error of at most 0.0042.
Values may be sent and summed in bfloat16 or wider, within the bound.
A program may use at most 64 MiB of HBM per device.

```python
import jax
import jax.numpy as jnp
from jax import lax

W = 1024
ROWS = 128
ROUNDS = 3
TOTAL = 16384
N_ROW = 8
N_COL = 16


def draw_opponent_tile(key, part):
    key = jax.random.fold_in(key, 7)
    first, second = jax.random.split(key)
    blocks = N_ROW * N_COL
    order = jax.random.permutation(first, blocks).astype(jnp.int32)
    start = jax.random.randint(second, (), 0, blocks - 1).astype(jnp.int32)
    labels = jnp.arange(blocks - 1, dtype=jnp.int32)
    rounds = []
    for step in range(ROUNDS):
        centre = (start + step) % (blocks - 1)
        other = (2 * centre - labels) % (blocks - 1)
        other = jnp.where(other == labels, blocks - 1, other)
        mates = jnp.concatenate([other, centre[None]]).astype(jnp.int32)
        rounds.append(jnp.zeros((blocks,), jnp.int32).at[order].set(order[mates]))
    return jnp.stack(rounds)


def touch_ends(entries, rng, least, high):
    shape = entries.shape
    place = [jax.random.randint(jax.random.fold_in(rng, axis), (), 0, shape[axis]) for axis in range(len(shape))]
    entries = entries.at[tuple(place)].set(least)
    longest = shape.index(max(shape))
    place[longest] = (place[longest] + 1) % shape[longest]
    return entries.at[tuple(place)].set(high)


def shard_levels(rng, dims, cuts, low, largest):
    factor_of = 1.0
    for position, blocks in cuts:
        steps = jax.random.uniform(jax.random.fold_in(jax.random.fold_in(rng, 6), position), (blocks,), jnp.float32, low / len(cuts), largest / len(cuts))
        factor_of = factor_of * jnp.repeat(jnp.exp(steps), dims[position] // blocks).reshape((-1,) + (1,) * (len(dims) - 1 - position))
    return factor_of


def gaussian(own_key, shape, scale, bound, cuts=(), kind=jnp.bfloat16):
    values = jax.random.normal(own_key, shape, jnp.float32) * scale
    if len(cuts) > 0:
        values = shard_levels(own_key, shape, cuts, -0.22, 0.18) * values
    return jnp.clip(values, min=-bound, max=bound).astype(kind)


def setup_inputs(seed: int = 0) -> dict:
    seeds = jax.random.split(jax.random.key(seed), 8)
    anchor_features = gaussian(seeds[0], (TOTAL, W), 1.0, 6.0, ((0, 128),), jnp.float32)
    candidate_features = gaussian(seeds[1], (TOTAL, W), 1.0, 6.0, ((0, 128),), jnp.float32)
    anchor_sample_ids = touch_ends(jax.random.randint(seeds[2], (TOTAL,), 0, TOTAL // 4), jax.random.fold_in(seeds[2], 1), 0, (TOTAL // 4) - 1).astype(jnp.int32)
    candidate_sample_ids = touch_ends(jax.random.randint(seeds[3], (TOTAL,), 0, TOTAL // 4), jax.random.fold_in(seeds[3], 1), 0, (TOTAL // 4) - 1).astype(jnp.int32)
    opponent_tile = draw_opponent_tile(jax.random.fold_in(seeds[7], 71), 0)
    sharpness_array = jnp.clip(jax.random.uniform(seeds[5], (1,), jnp.float32, 8.0, 16.0), 8.0, 16.0)
    score_offset = jnp.clip(jax.random.uniform(seeds[6], (1,), jnp.float32, -3.0, 0.0), -3.0, 0.0)
    return dict(anchor_features=anchor_features, candidate_features=candidate_features, anchor_sample_ids=anchor_sample_ids, candidate_sample_ids=candidate_sample_ids, opponent_tile=opponent_tile, sharpness_array=sharpness_array, score_offset=score_offset)


def normalize(embed):
    sharpness_factor = lax.rsqrt(lax.optimization_barrier(jnp.sum(embed * embed, axis=-1, keepdims=True)) + 1e-06)
    return (embed * sharpness_factor).astype(jnp.bfloat16)

def tile_derivative_fn(anchor_tile_vectors, candidate_tile_vectors, anchor_tile_ids, candidate_tile_ids, sharpness_array, score_offset):
    positive_target = jnp.where(anchor_tile_ids[:, None] == candidate_tile_ids[None, :], 1.0, -1.0).astype(jnp.float32)
    similarity_table = sharpness_array * jnp.dot(anchor_tile_vectors, candidate_tile_vectors.T, preferred_element_type=jnp.float32) + score_offset
    return (-sharpness_array * positive_target * jax.nn.sigmoid(-positive_target * similarity_table)).astype(jnp.bfloat16)

def reference(anchor_features, candidate_features, anchor_sample_ids, candidate_sample_ids, opponent_tile, sharpness_array, score_offset):
    blocks = N_ROW * N_COL
    a_hat = normalize(anchor_features).reshape(blocks, ROWS, W)
    b_hat = normalize(candidate_features).reshape(blocks, ROWS, W)
    ida = anchor_sample_ids.reshape(blocks, ROWS)
    idb = candidate_sample_ids.reshape(blocks, ROWS)
    sharpness_factor = sharpness_array[0]
    shift = score_offset[0]

    def one_block(index):
        own_a = a_hat[index]
        own_b = b_hat[index]
        slope = tile_derivative_fn(own_a, own_b, ida[index], idb[index], sharpness_factor, shift)
        total_a = jnp.dot(slope, own_b, preferred_element_type=jnp.float32)
        total_b = jnp.dot(slope.T, own_a, preferred_element_type=jnp.float32)
        for step in range(ROUNDS):
            other = opponent_tile[step, index].astype(jnp.int32)
            far_a = a_hat[other]
            far_b = b_hat[other]
            slope = tile_derivative_fn(own_a, far_b, ida[index], idb[other], sharpness_factor, shift)
            total_a = total_a + jnp.dot(slope, far_b, preferred_element_type=jnp.float32)
            mirror = tile_derivative_fn(far_a, own_b, ida[other], idb[index], sharpness_factor, shift)
            total_b = total_b + jnp.dot(mirror.T, far_a, preferred_element_type=jnp.float32)
        return (total_a, total_b)
    grads_a, grads_b = lax.map(one_block, jnp.arange(blocks, dtype=jnp.int32))
    return (grads_a.reshape(TOTAL, W), grads_b.reshape(TOTAL, W))
```

```python
import functools
import random

import jax
import jax.numpy as jnp
from jax import lax
from jax.experimental import pallas as pl
from jax.experimental.pallas import tpu as pltpu
from jax.sharding import PartitionSpec as P

LOGICAL = pl.DeviceIdType.LOGICAL
CHIPS = 4
TILE = (16, 128)


def far_first():
    offsets = [
        (dx, dy, dz, dc)
        for dx in range(CHIPS)
        for dy in range(CHIPS)
        for dz in range(CHIPS)
        for dc in range(2)
    ][1:]
    random.Random(1).shuffle(offsets)
    offsets.sort(key=lambda o: -sum(min(d, CHIPS - d) for d in o[:3]))
    return offsets


def kernel(
    a_ref,
    b_ref,
    ida_ref,
    idb_ref,
    opponent_ref,
    sharpness_ref,
    offset_ref,
    grad_a_ref,
    grad_b_ref,
    raw,
    own,
    mid,
    out,
    far,
    load_sem,
    send_sem,
    recv_sem,
):
    rounds = opponent_ref.shape[0]
    loads = [
        pltpu.make_async_copy(src, raw.at[side], load_sem.at[side])
        for side, src in enumerate((a_ref, b_ref))
    ]
    for load in loads:
        load.start()

    row, col = lax.axis_index("row"), lax.axis_index("col")
    x, z_lo = row % CHIPS, row // CHIPS
    y, z_hi, core = col // CHIPS, (col // 2) % 2, col % 2
    z = z_hi * 2 + z_lo
    me = row * 16 + col

    xs = [(x + d) % CHIPS for d in range(CHIPS)]
    ys = [(y + d) % CHIPS for d in range(CHIPS)]
    zs = [(z + d) % CHIPS for d in range(CHIPS)]
    cs = [core, 1 - core]
    index_x = [v * 16 for v in xs]
    index_y = [v * 4 for v in ys]
    index_z = [(v % 2) * 64 + (v // 2) * 2 for v in zs]
    group_z = [v * 4 for v in zs]
    group_y = [v * 2 for v in ys]

    def device(o):
        return index_x[o[0]] + index_y[o[1]] + index_z[o[2]] + cs[o[3]]

    def tile_of(o):
        return group_z[o[2]] + xs[o[0]], group_y[o[1]] + cs[o[3]]

    others = far_first()
    barrier = pltpu.get_barrier_semaphore()
    for o in others:
        pl.semaphore_signal(barrier, inc=1, device_id=device(o), device_id_type=LOGICAL)

    for side in range(2):
        loads[side].wait()
        for g in range(8):
            value = raw[side, pl.ds(g * 16, 16), :]
            scale = lax.rsqrt(jnp.sum(value * value, axis=-1, keepdims=True) + 1e-06)
            value = (value * scale).astype(jnp.bfloat16)
            for c in range(8):
                own[side * 8 + g, c] = value[:, c * 128 : (c + 1) * 128]

    pl.semaphore_wait(barrier, len(others))

    for o in others:
        g, c = tile_of(o)
        pltpu.make_async_remote_copy(
            src_ref=own.at[g, c],
            dst_ref=mid.at[me],
            send_sem=send_sem.at[0],
            recv_sem=recv_sem.at[0],
            device_id=device(o),
            device_id_type=LOGICAL,
        ).start()
    my_g, my_c = tile_of((0, 0, 0, 0))
    mid[me] = own[my_g, my_c]

    sharpness = sharpness_ref[0]
    shift = offset_ref[0]

    def block(ref, side, k=None):
        def column(c):
            part = ref[side * 8 : side * 8 + 8, c] if k is None else ref[side * 8 : side * 8 + 8, c, k]
            return part.reshape(128, 128)
        return [jnp.concatenate([column(2 * j), column(2 * j + 1)], axis=1) for j in range(4)]

    def slope(mine, theirs, my_ids, their_ids):
        score = jnp.zeros((128, 128), jnp.float32)
        for p, q in zip(mine, theirs):
            score += lax.dot_general(p, q, (((1,), (1,)), ((), ())), preferred_element_type=jnp.float32)
        label = jnp.where(my_ids == their_ids, 1.0, -1.0).astype(jnp.float32)
        logit = sharpness * score + shift
        return (-sharpness * label * jax.nn.sigmoid(-label * logit)).astype(jnp.bfloat16)

    ids = (ida_ref, idb_ref)
    grads = (grad_a_ref, grad_b_ref)
    my_ids = []
    for side in range(2):
        line = ids[side][pl.ds(me, 1), :]
        my_ids.append(jnp.transpose(jnp.broadcast_to(line, (128, 128))))
    for side in range(2):
        theirs = block(own, 1 - side)
        g = slope(block(own, side), theirs, my_ids[side], ids[1 - side][pl.ds(me, 1), :])
        for j in range(4):
            grads[side][:, j * 256 : (j + 1) * 256] = jnp.dot(g, theirs[j], preferred_element_type=jnp.float32)

    landed = mid.at[pl.ds(0, len(others))]
    pltpu.make_async_copy(landed, landed, recv_sem.at[0]).wait()

    for o in others:
        there = device(o)
        for k in range(rounds):
            out[there, k] = mid[opponent_ref[k, there]]
        pltpu.make_async_remote_copy(
            src_ref=out.at[there],
            dst_ref=far.at[my_g, my_c],
            send_sem=send_sem.at[1],
            recv_sem=recv_sem.at[1],
            device_id=there,
            device_id_type=LOGICAL,
        ).start()
    for k in range(rounds):
        far[my_g, my_c, k] = mid[opponent_ref[k, me]]

    sent = out.at[pl.ds(0, len(others))]
    pltpu.make_async_copy(sent, sent, recv_sem.at[1]).wait()

    for side in range(2):
        mine = block(own, side)
        theirs = [block(far, 1 - side, k) for k in range(rounds)]
        g = jnp.concatenate(
            [
                slope(mine, theirs[k], my_ids[side], ids[1 - side][pl.ds(opponent_ref[k, me], 1), :])
                for k in range(rounds)
            ],
            axis=1,
        )
        for j in range(4):
            slab = jnp.concatenate([theirs[k][j] for k in range(rounds)], axis=0)
            grads[side][:, j * 256 : (j + 1) * 256] += jnp.dot(g, slab, preferred_element_type=jnp.float32)

    pltpu.make_async_copy(landed, landed, send_sem.at[0]).wait()
    pltpu.make_async_copy(sent, sent, send_sem.at[1]).wait()


def shards(
    anchor_features,
    candidate_features,
    anchor_sample_ids,
    candidate_sample_ids,
    opponent_tile,
    sharpness_array,
    score_offset,
):
    rows, width = anchor_features.shape
    rounds, blocks = opponent_tile.shape
    anywhere = pl.BlockSpec(memory_space=pl.ANY)
    vmem = pl.BlockSpec(memory_space=pltpu.VMEM)
    smem = pl.BlockSpec(memory_space=pltpu.SMEM)
    grad = jax.ShapeDtypeStruct((rows, width), jnp.float32)
    return pl.pallas_call(
        kernel,
        out_shape=(grad, grad),
        in_specs=[anywhere, anywhere, vmem, vmem, smem, smem, smem],
        out_specs=(vmem, vmem),
        scratch_shapes=[
            pltpu.VMEM((2, rows, width), jnp.float32),
            pltpu.VMEM((16, 8) + TILE, jnp.bfloat16),
            pltpu.VMEM((blocks,) + TILE, jnp.bfloat16),
            pltpu.VMEM((blocks, rounds) + TILE, jnp.bfloat16),
            pltpu.VMEM((16, 8, rounds) + TILE, jnp.bfloat16),
            pltpu.SemaphoreType.DMA((2,)),
            pltpu.SemaphoreType.DMA((2,)),
            pltpu.SemaphoreType.DMA((2,)),
        ],
        compiler_params=pltpu.CompilerParams(
            collective_id=0, has_side_effects=True, vmem_limit_bytes=32 * 1024 * 1024
        ),
        name="spread_deliver",
    )(
        anchor_features,
        candidate_features,
        anchor_sample_ids.reshape(blocks, rows),
        candidate_sample_ids.reshape(blocks, rows),
        opponent_tile,
        sharpness_array,
        score_offset,
    )


def solution(mesh):
    placed = (P(("row", "col"), None), P(("row", "col"), None), P(), P(), P(), P(), P())
    return jax.shard_map(
        shards,
        mesh=mesh,
        in_specs=placed,
        out_specs=(P(("row", "col"), None), P(("row", "col"), None)),
        check_vma=False,
    )
```

```python
import functools
import random

import jax
import jax.numpy as jnp
from jax import lax
from jax.experimental import pallas as pl
from jax.experimental.pallas import tpu as pltpu
from jax.sharding import PartitionSpec as P

LOGICAL = pl.DeviceIdType.LOGICAL
CHIPS = 4
TILE = (16, 128)


def in_hbm(array):
    return pltpu.with_memory_space_constraint(array, pltpu.HBM)


def far_first():
    offsets = [
        (dx, dy, dz, dc)
        for dx in range(CHIPS)
        for dy in range(CHIPS)
        for dz in range(CHIPS)
        for dc in range(2)
    ][1:]
    random.Random(1).shuffle(offsets)
    offsets.sort(key=lambda o: -sum(min(d, CHIPS - d) for d in o[:3]))
    return offsets


def kernel(
    a_ref,
    b_ref,
    ida_ref,
    idb_ref,
    opponent_hbm,
    sharpness_ref,
    offset_ref,
    grad_a_ref,
    grad_b_ref,
    raw,
    ids,
    opponent_ref,
    own,
    mid,
    out,
    far,
    load_sem,
    send_sem,
    recv_sem,
):
    rounds = opponent_ref.shape[0]
    loads = [
        pltpu.make_async_copy(src, dst, load_sem.at[i])
        for i, (src, dst) in enumerate(
            (
                (a_ref, raw.at[0]),
                (b_ref, raw.at[1]),
                (ida_ref, ids.at[0]),
                (idb_ref, ids.at[1]),
                (opponent_hbm, opponent_ref),
            )
        )
    ]
    for load in loads:
        load.start()

    row, col = lax.axis_index("row"), lax.axis_index("col")
    x, z_lo = row % CHIPS, row // CHIPS
    y, z_hi, core = col // CHIPS, (col // 2) % 2, col % 2
    z = z_hi * 2 + z_lo
    me = row * 16 + col

    xs = [(x + d) % CHIPS for d in range(CHIPS)]
    ys = [(y + d) % CHIPS for d in range(CHIPS)]
    zs = [(z + d) % CHIPS for d in range(CHIPS)]
    cs = [core, 1 - core]
    index_x = [v * 16 for v in xs]
    index_y = [v * 4 for v in ys]
    index_z = [(v % 2) * 64 + (v // 2) * 2 for v in zs]
    group_z = [v * 4 for v in zs]
    group_y = [v * 2 for v in ys]

    def device(o):
        return index_x[o[0]] + index_y[o[1]] + index_z[o[2]] + cs[o[3]]

    def tile_of(o):
        return group_z[o[2]] + xs[o[0]], group_y[o[1]] + cs[o[3]]

    others = far_first()
    barrier = pltpu.get_barrier_semaphore()
    for o in others:
        pl.semaphore_signal(barrier, inc=1, device_id=device(o), device_id_type=LOGICAL)

    for side in range(2):
        loads[side].wait()
        for g in range(8):
            value = raw[side, pl.ds(g * 16, 16), :]
            scale = lax.rsqrt(jnp.sum(value * value, axis=-1, keepdims=True) + 1e-06)
            value = (value * scale).astype(jnp.bfloat16)
            for c in range(8):
                own[side * 8 + g, c] = value[:, c * 128 : (c + 1) * 128]

    pl.semaphore_wait(barrier, len(others))

    for o in others:
        g, c = tile_of(o)
        pltpu.make_async_remote_copy(
            src_ref=own.at[g, c],
            dst_ref=mid.at[me],
            send_sem=send_sem.at[0],
            recv_sem=recv_sem.at[0],
            device_id=device(o),
            device_id_type=LOGICAL,
        ).start()
    my_g, my_c = tile_of((0, 0, 0, 0))
    mid[me] = own[my_g, my_c]

    sharpness = sharpness_ref[0]
    shift = offset_ref[0]

    def block(ref, side, k=None):
        def column(c):
            part = ref[side * 8 : side * 8 + 8, c] if k is None else ref[side * 8 : side * 8 + 8, c, k]
            return part.reshape(128, 128)
        return [jnp.concatenate([column(2 * j), column(2 * j + 1)], axis=1) for j in range(4)]

    def slope(mine, theirs, my_ids, their_ids):
        score = jnp.zeros((128, 128), jnp.float32)
        for p, q in zip(mine, theirs):
            score += lax.dot_general(p, q, (((1,), (1,)), ((), ())), preferred_element_type=jnp.float32)
        label = jnp.where(my_ids == their_ids, 1.0, -1.0).astype(jnp.float32)
        logit = sharpness * score + shift
        return (-sharpness * label * jax.nn.sigmoid(-label * logit)).astype(jnp.bfloat16)

    for load in loads[2:]:
        load.wait()
    grads = (grad_a_ref, grad_b_ref)
    my_ids = []
    for side in range(2):
        line = ids[side, pl.ds(me, 1), :]
        my_ids.append(jnp.transpose(jnp.broadcast_to(line, (128, 128))))
    for side in range(2):
        theirs = block(own, 1 - side)
        g = slope(block(own, side), theirs, my_ids[side], ids[1 - side, pl.ds(me, 1), :])
        for j in range(4):
            grads[side][:, j * 256 : (j + 1) * 256] = jnp.dot(g, theirs[j], preferred_element_type=jnp.float32)

    landed = mid.at[pl.ds(0, len(others))]
    pltpu.make_async_copy(landed, landed, recv_sem.at[0]).wait()

    for o in others:
        there = device(o)
        for k in range(rounds):
            out[there, k] = mid[opponent_ref[k, there]]
        pltpu.make_async_remote_copy(
            src_ref=out.at[there],
            dst_ref=far.at[my_g, my_c],
            send_sem=send_sem.at[1],
            recv_sem=recv_sem.at[1],
            device_id=there,
            device_id_type=LOGICAL,
        ).start()
    for k in range(rounds):
        far[my_g, my_c, k] = mid[opponent_ref[k, me]]

    sent = out.at[pl.ds(0, len(others))]
    pltpu.make_async_copy(sent, sent, recv_sem.at[1]).wait()

    for side in range(2):
        mine = block(own, side)
        theirs = [block(far, 1 - side, k) for k in range(rounds)]
        g = jnp.concatenate(
            [
                slope(mine, theirs[k], my_ids[side], ids[1 - side, pl.ds(opponent_ref[k, me], 1), :])
                for k in range(rounds)
            ],
            axis=1,
        )
        for j in range(4):
            slab = jnp.concatenate([theirs[k][j] for k in range(rounds)], axis=0)
            grads[side][:, j * 256 : (j + 1) * 256] += jnp.dot(g, slab, preferred_element_type=jnp.float32)

    pltpu.make_async_copy(landed, landed, send_sem.at[0]).wait()
    pltpu.make_async_copy(sent, sent, send_sem.at[1]).wait()


def shards(
    anchor_features,
    candidate_features,
    anchor_sample_ids,
    candidate_sample_ids,
    opponent_tile,
    sharpness_array,
    score_offset,
):
    rows, width = anchor_features.shape
    rounds, blocks = opponent_tile.shape
    hbm = pl.BlockSpec(memory_space=pltpu.HBM)
    vmem = pl.BlockSpec(memory_space=pltpu.VMEM)
    smem = pl.BlockSpec(memory_space=pltpu.SMEM)
    grad = jax.ShapeDtypeStruct((rows, width), jnp.float32)
    return pl.pallas_call(
        kernel,
        out_shape=(grad, grad),
        in_specs=[hbm, hbm, hbm, hbm, hbm, smem, smem],
        out_specs=(vmem, vmem),
        scratch_shapes=[
            pltpu.VMEM((2, rows, width), jnp.float32),
            pltpu.VMEM((2, blocks, rows), jnp.int32),
            pltpu.SMEM((rounds, blocks), jnp.int32),
            pltpu.VMEM((16, 8) + TILE, jnp.bfloat16),
            pltpu.VMEM((blocks,) + TILE, jnp.bfloat16),
            pltpu.VMEM((blocks, rounds) + TILE, jnp.bfloat16),
            pltpu.VMEM((16, 8, rounds) + TILE, jnp.bfloat16),
            pltpu.SemaphoreType.DMA((5,)),
            pltpu.SemaphoreType.DMA((2,)),
            pltpu.SemaphoreType.DMA((2,)),
        ],
        compiler_params=pltpu.CompilerParams(
            collective_id=0, has_side_effects=True, vmem_limit_bytes=32 * 1024 * 1024
        ),
        name="spread_deliver",
    )(
        in_hbm(anchor_features),
        in_hbm(candidate_features),
        in_hbm(anchor_sample_ids.reshape(blocks, rows)),
        in_hbm(candidate_sample_ids.reshape(blocks, rows)),
        in_hbm(opponent_tile),
        sharpness_array,
        score_offset,
    )


def solution(mesh):
    placed = (P(("row", "col"), None), P(("row", "col"), None), P(), P(), P(), P(), P())
    return jax.shard_map(
        shards,
        mesh=mesh,
        in_specs=placed,
        out_specs=(P(("row", "col"), None), P(("row", "col"), None)),
        check_vma=False,
    )
```

```python
import functools
import random

import jax
import jax.numpy as jnp
from jax import lax
from jax.experimental import pallas as pl
from jax.experimental.pallas import tpu as pltpu
from jax.sharding import PartitionSpec as P

LOGICAL = pl.DeviceIdType.LOGICAL
CHIPS = 4
TILE = (16, 128)


def in_hbm(array):
    return pltpu.with_memory_space_constraint(array, pltpu.HBM)


def far_first():
    offsets = [(dx, dy, dz) for dx in range(CHIPS) for dy in range(CHIPS) for dz in range(CHIPS)][1:]
    random.Random(1).shuffle(offsets)
    offsets.sort(key=lambda o: -sum(min(d, CHIPS - d) for d in o))
    return offsets


def kernel(
    a_ref,
    b_ref,
    ida_ref,
    idb_ref,
    opponent_hbm,
    sharpness_ref,
    offset_ref,
    grad_a_ref,
    grad_b_ref,
    raw,
    ids,
    opponent_ref,
    own,
    mid,
    out,
    far,
    load_sem,
    send_sem,
    recv_sem,
):
    rounds = opponent_ref.shape[0]
    loads = [
        pltpu.make_async_copy(src, dst, load_sem.at[i])
        for i, (src, dst) in enumerate(
            (
                (a_ref, raw.at[0]),
                (b_ref, raw.at[1]),
                (ida_ref, ids.at[0]),
                (idb_ref, ids.at[1]),
                (opponent_hbm, opponent_ref),
            )
        )
    ]
    for load in loads:
        load.start()

    row, col = lax.axis_index("row"), lax.axis_index("col")
    x, z_lo = row % CHIPS, row // CHIPS
    y, z_hi, core = col // CHIPS, (col // 2) % 2, col % 2
    z = z_hi * 2 + z_lo
    me = row * 16 + col

    xs = [(x + d) % CHIPS for d in range(CHIPS)]
    ys = [(y + d) % CHIPS for d in range(CHIPS)]
    zs = [(z + d) % CHIPS for d in range(CHIPS)]
    index_x = [v * 16 for v in xs]
    index_y = [v * 4 for v in ys]
    index_z = [(v % 2) * 64 + (v // 2) * 2 for v in zs]
    group_x = [v // 2 for v in xs]
    group_z = [v * 2 for v in zs]
    column_x = [(v % 2) * 4 for v in xs]

    def device(o):
        return index_x[o[0]] + index_y[o[1]] + index_z[o[2]] + o[3]

    def tile_of(o):
        return o[3], group_z[o[2]] + group_x[o[0]], column_x[o[0]] + ys[o[1]]

    chips = far_first()
    here, beside = (0, 0, 0, core), (0, 0, 0, 1 - core)
    spread = [beside] + [o + (c,) for c in range(2) for o in chips]
    deliver = [o + (c,) for c in range(2) for o in chips] + [beside]
    barrier = pltpu.get_barrier_semaphore()
    for o in deliver:
        pl.semaphore_signal(barrier, inc=1, device_id=device(o), device_id_type=LOGICAL)

    for side in range(2):
        loads[side].wait()
        for g in range(8):
            value = raw[side, pl.ds(g * 16, 16), :]
            scale = lax.rsqrt(jnp.sum(value * value, axis=-1, keepdims=True) + 1e-06)
            value = (value * scale).astype(jnp.bfloat16)
            for c in range(8):
                own[side, g, c] = value[:, c * 128 : (c + 1) * 128]

    pl.semaphore_wait(barrier, len(deliver))

    for o in spread:
        pltpu.make_async_remote_copy(
            src_ref=own.at[tile_of(o)],
            dst_ref=mid.at[me],
            send_sem=send_sem.at[0],
            recv_sem=recv_sem.at[0],
            device_id=device(o),
            device_id_type=LOGICAL,
        ).start()
    my_tile = tile_of(here)
    pltpu.make_async_copy(own.at[my_tile], mid.at[me], recv_sem.at[0]).start()

    sharpness = sharpness_ref[0]
    shift = offset_ref[0]

    def block(ref, side, k=None):
        def column(c):
            part = ref[side, :, c] if k is None else ref[side, :, c, k]
            return part.reshape(128, 128)
        return [jnp.concatenate([column(2 * j), column(2 * j + 1)], axis=1) for j in range(4)]

    def slope(mine, theirs, my_ids, their_ids):
        score = jnp.zeros((128, 128), jnp.float32)
        for p, q in zip(mine, theirs):
            score += lax.dot_general(p, q, (((1,), (1,)), ((), ())), preferred_element_type=jnp.float32)
        label = jnp.where(my_ids == their_ids, 1.0, -1.0).astype(jnp.float32)
        logit = sharpness * score + shift
        return (-sharpness * label * jax.nn.sigmoid(-label * logit)).astype(jnp.bfloat16)

    for load in loads[2:]:
        load.wait()
    grads = (grad_a_ref, grad_b_ref)
    my_ids = []
    for side in range(2):
        line = ids[side, pl.ds(me, 1), :]
        my_ids.append(jnp.transpose(jnp.broadcast_to(line, (128, 128))))
    for side in range(2):
        theirs = block(own, 1 - side)
        g = slope(block(own, side), theirs, my_ids[side], ids[1 - side, pl.ds(me, 1), :])
        for j in range(4):
            grads[side][:, j * 256 : (j + 1) * 256] = jnp.dot(g, theirs[j], preferred_element_type=jnp.float32)

    pltpu.make_async_copy(mid, mid, recv_sem.at[0]).wait()

    def fetch(there):
        for k in range(rounds):
            out[there, k] = mid[opponent_ref[k, there]]

    for o in deliver:
        there = device(o)
        fetch(there)
        pltpu.make_async_remote_copy(
            src_ref=out.at[there],
            dst_ref=far.at[my_tile],
            send_sem=send_sem.at[1],
            recv_sem=recv_sem.at[1 + core],
            device_id=there,
            device_id_type=LOGICAL,
        ).start()
    fetch(me)
    pltpu.make_async_copy(out.at[me], far.at[my_tile], recv_sem.at[1 + core]).start()

    for side in (1, 0):
        arrived = far.at[1 - side]
        pltpu.make_async_copy(arrived, arrived, recv_sem.at[2 - side]).wait()
        mine = block(own, side)
        theirs = [block(far, 1 - side, k) for k in range(rounds)]
        g = jnp.concatenate(
            [
                slope(mine, theirs[k], my_ids[side], ids[1 - side, pl.ds(opponent_ref[k, me], 1), :])
                for k in range(rounds)
            ],
            axis=1,
        )
        for j in range(4):
            slab = jnp.concatenate([theirs[k][j] for k in range(rounds)], axis=0)
            grads[side][:, j * 256 : (j + 1) * 256] += jnp.dot(g, slab, preferred_element_type=jnp.float32)

    spread_out = mid.at[pl.ds(0, len(spread))]
    pltpu.make_async_copy(spread_out, spread_out, send_sem.at[0]).wait()
    sent = out.at[pl.ds(0, len(deliver))]
    pltpu.make_async_copy(sent, sent, send_sem.at[1]).wait()


def store(in_a, in_b, out_a, out_b, sem):
    copies = [
        pltpu.make_async_copy(src, dst, sem.at[side])
        for side, (src, dst) in enumerate(((in_a, out_a), (in_b, out_b)))
    ]
    for copy in copies:
        copy.start()
    for copy in copies:
        copy.wait()


def shards(
    anchor_features,
    candidate_features,
    anchor_sample_ids,
    candidate_sample_ids,
    opponent_tile,
    sharpness_array,
    score_offset,
):
    rows, width = anchor_features.shape
    rounds, blocks = opponent_tile.shape
    hbm = pl.BlockSpec(memory_space=pltpu.HBM)
    vmem = pl.BlockSpec(memory_space=pltpu.VMEM)
    smem = pl.BlockSpec(memory_space=pltpu.SMEM)
    grad = jax.ShapeDtypeStruct((rows, width), jnp.float32)
    grads = pl.pallas_call(
        kernel,
        out_shape=(grad, grad),
        in_specs=[hbm, hbm, hbm, hbm, hbm, smem, smem],
        out_specs=(vmem, vmem),
        scratch_shapes=[
            pltpu.VMEM((2, rows, width), jnp.float32),
            pltpu.VMEM((2, blocks, rows), jnp.int32),
            pltpu.SMEM((rounds, blocks), jnp.int32),
            pltpu.VMEM((2, 8, 8) + TILE, jnp.bfloat16),
            pltpu.VMEM((blocks,) + TILE, jnp.bfloat16),
            pltpu.VMEM((blocks, rounds) + TILE, jnp.bfloat16),
            pltpu.VMEM((2, 8, 8, rounds) + TILE, jnp.bfloat16),
            pltpu.SemaphoreType.DMA((5,)),
            pltpu.SemaphoreType.DMA((2,)),
            pltpu.SemaphoreType.DMA((3,)),
        ],
        compiler_params=pltpu.CompilerParams(
            collective_id=0, has_side_effects=True, vmem_limit_bytes=32 * 1024 * 1024
        ),
        name="spread_deliver",
    )(
        in_hbm(anchor_features),
        in_hbm(candidate_features),
        in_hbm(anchor_sample_ids.reshape(blocks, rows)),
        in_hbm(candidate_sample_ids.reshape(blocks, rows)),
        in_hbm(opponent_tile),
        sharpness_array,
        score_offset,
    )
    return pl.pallas_call(
        store,
        out_shape=(grad, grad),
        in_specs=[vmem, vmem],
        out_specs=(hbm, hbm),
        scratch_shapes=[pltpu.SemaphoreType.DMA((2,))],
        name="store",
    )(*[pltpu.with_memory_space_constraint(g, pltpu.VMEM) for g in grads])


def solution(mesh):
    placed = (P(("row", "col"), None), P(("row", "col"), None), P(), P(), P(), P(), P())
    return jax.shard_map(
        shards,
        mesh=mesh,
        in_specs=placed,
        out_specs=(P(("row", "col"), None), P(("row", "col"), None)),
        check_vma=False,
    )
```

```python
import functools
import random

import jax
import jax.numpy as jnp
from jax import lax
from jax.experimental import pallas as pl
from jax.experimental.pallas import tpu as pltpu
from jax.sharding import PartitionSpec as P

LOGICAL = pl.DeviceIdType.LOGICAL
CHIPS = 4
TILE = (16, 128)


def in_hbm(array):
    return pltpu.with_memory_space_constraint(array, pltpu.HBM)


def far_first():
    offsets = [(dx, dy, dz) for dx in range(CHIPS) for dy in range(CHIPS) for dz in range(CHIPS)][1:]
    random.Random(1).shuffle(offsets)
    offsets.sort(key=lambda o: -sum(min(d, CHIPS - d) for d in o))
    return offsets


def kernel(
    a_ref,
    b_ref,
    ida_ref,
    idb_ref,
    opponent_hbm,
    sharpness_ref,
    offset_ref,
    grad_a_ref,
    grad_b_ref,
    raw,
    ids,
    opponent_ref,
    own,
    mid,
    out,
    far,
    load_sem,
    send_sem,
    recv_sem,
):
    rounds = opponent_ref.shape[0]
    loads = [
        pltpu.make_async_copy(src, dst, load_sem.at[i])
        for i, (src, dst) in enumerate(
            (
                (a_ref, raw.at[0]),
                (b_ref, raw.at[1]),
                (ida_ref, ids.at[0]),
                (idb_ref, ids.at[1]),
                (opponent_hbm, opponent_ref),
            )
        )
    ]
    for load in loads:
        load.start()

    row, col = lax.axis_index("row"), lax.axis_index("col")
    x, z_lo = row % CHIPS, row // CHIPS
    y, z_hi, core = col // CHIPS, (col // 2) % 2, col % 2
    z = z_hi * 2 + z_lo
    me = row * 16 + col

    xs = [(x + d) % CHIPS for d in range(CHIPS)]
    ys = [(y + d) % CHIPS for d in range(CHIPS)]
    zs = [(z + d) % CHIPS for d in range(CHIPS)]
    index_x = [v * 16 for v in xs]
    index_y = [v * 4 for v in ys]
    index_z = [(v % 2) * 64 + (v // 2) * 2 for v in zs]
    group_x = [v // 2 for v in xs]
    group_z = [v * 2 for v in zs]
    column_x = [(v % 2) * 4 for v in xs]

    def device(o):
        return index_x[o[0]] + index_y[o[1]] + index_z[o[2]] + o[3]

    def tile_of(o):
        return o[3], group_z[o[2]] + group_x[o[0]], column_x[o[0]] + ys[o[1]]

    chips = far_first()
    here, beside = (0, 0, 0, core), (0, 0, 0, 1 - core)
    spread = [beside] + [o + (c,) for c in range(2) for o in chips]
    deliver = [o + (c,) for c in (1, 0) for o in chips] + [beside]
    barrier = pltpu.get_barrier_semaphore()
    for o in [o + (c,) for o in chips for c in range(2)] + [beside]:
        pl.semaphore_signal(barrier, inc=1, device_id=device(o), device_id_type=LOGICAL)

    for side in range(2):
        loads[side].wait()
        for g in range(8):
            value = raw[side, pl.ds(g * 16, 16), :]
            scale = lax.rsqrt(jnp.sum(value * value, axis=-1, keepdims=True) + 1e-06)
            value = (value * scale).astype(jnp.bfloat16)
            for c in range(8):
                own[side, g, c] = value[:, c * 128 : (c + 1) * 128]

    pl.semaphore_wait(barrier, len(deliver))

    for o in spread:
        pltpu.make_async_remote_copy(
            src_ref=own.at[tile_of(o)],
            dst_ref=mid.at[me],
            send_sem=send_sem.at[0],
            recv_sem=recv_sem.at[0],
            device_id=device(o),
            device_id_type=LOGICAL,
        ).start()
    my_tile = tile_of(here)
    pltpu.make_async_copy(own.at[my_tile], mid.at[me], recv_sem.at[0]).start()

    sharpness = sharpness_ref[0]
    shift = offset_ref[0]

    def block(ref, side, k=None):
        def column(c):
            part = ref[side, :, c] if k is None else ref[side, :, c, k]
            return part.reshape(128, 128)
        return [jnp.concatenate([column(2 * j), column(2 * j + 1)], axis=1) for j in range(4)]

    def slope(mine, theirs, my_ids, their_ids):
        score = jnp.zeros((128, 128), jnp.float32)
        for p, q in zip(mine, theirs):
            score += lax.dot_general(p, q, (((1,), (1,)), ((), ())), preferred_element_type=jnp.float32)
        label = jnp.where(my_ids == their_ids, 1.0, -1.0).astype(jnp.float32)
        logit = sharpness * score + shift
        return (-sharpness * label * jax.nn.sigmoid(-label * logit)).astype(jnp.bfloat16)

    for load in loads[2:]:
        load.wait()
    grads = (grad_a_ref, grad_b_ref)
    my_ids = []
    for side in range(2):
        line = ids[side, pl.ds(me, 1), :]
        my_ids.append(jnp.transpose(jnp.broadcast_to(line, (128, 128))))
    for side in range(2):
        theirs = block(own, 1 - side)
        g = slope(block(own, side), theirs, my_ids[side], ids[1 - side, pl.ds(me, 1), :])
        for j in range(4):
            grads[side][:, j * 256 : (j + 1) * 256] = jnp.dot(g, theirs[j], preferred_element_type=jnp.float32)

    pltpu.make_async_copy(mid, mid, recv_sem.at[0]).wait()

    def fetch(there):
        for k in range(rounds):
            out[there, k] = mid[opponent_ref[k, there]]

    for o in deliver:
        there = device(o)
        fetch(there)
        pltpu.make_async_remote_copy(
            src_ref=out.at[there],
            dst_ref=far.at[my_tile],
            send_sem=send_sem.at[1],
            recv_sem=recv_sem.at[1 + core],
            device_id=there,
            device_id_type=LOGICAL,
        ).start()
    fetch(me)
    pltpu.make_async_copy(out.at[me], far.at[my_tile], recv_sem.at[1 + core]).start()

    for side in (1, 0):
        arrived = far.at[1 - side]
        pltpu.make_async_copy(arrived, arrived, recv_sem.at[2 - side]).wait()
        mine = block(own, side)
        theirs = [block(far, 1 - side, k) for k in range(rounds)]
        g = jnp.concatenate(
            [
                slope(mine, theirs[k], my_ids[side], ids[1 - side, pl.ds(opponent_ref[k, me], 1), :])
                for k in range(rounds)
            ],
            axis=1,
        )
        for j in range(4):
            slab = jnp.concatenate([theirs[k][j] for k in range(rounds)], axis=0)
            grads[side][:, j * 256 : (j + 1) * 256] += jnp.dot(g, slab, preferred_element_type=jnp.float32)

    spread_out = mid.at[pl.ds(0, len(spread))]
    pltpu.make_async_copy(spread_out, spread_out, send_sem.at[0]).wait()
    sent = out.at[pl.ds(0, len(deliver))]
    pltpu.make_async_copy(sent, sent, send_sem.at[1]).wait()


def store(in_a, in_b, out_a, out_b, sem):
    copies = [
        pltpu.make_async_copy(src, dst, sem.at[side])
        for side, (src, dst) in enumerate(((in_a, out_a), (in_b, out_b)))
    ]
    for copy in copies:
        copy.start()
    for copy in copies:
        copy.wait()


def shards(
    anchor_features,
    candidate_features,
    anchor_sample_ids,
    candidate_sample_ids,
    opponent_tile,
    sharpness_array,
    score_offset,
):
    rows, width = anchor_features.shape
    rounds, blocks = opponent_tile.shape
    hbm = pl.BlockSpec(memory_space=pltpu.HBM)
    vmem = pl.BlockSpec(memory_space=pltpu.VMEM)
    smem = pl.BlockSpec(memory_space=pltpu.SMEM)
    grad = jax.ShapeDtypeStruct((rows, width), jnp.float32)
    grads = pl.pallas_call(
        kernel,
        out_shape=(grad, grad),
        in_specs=[hbm, hbm, hbm, hbm, hbm, smem, smem],
        out_specs=(vmem, vmem),
        scratch_shapes=[
            pltpu.VMEM((2, rows, width), jnp.float32),
            pltpu.VMEM((2, blocks, rows), jnp.int32),
            pltpu.SMEM((rounds, blocks), jnp.int32),
            pltpu.VMEM((2, 8, 8) + TILE, jnp.bfloat16),
            pltpu.VMEM((blocks,) + TILE, jnp.bfloat16),
            pltpu.VMEM((blocks, rounds) + TILE, jnp.bfloat16),
            pltpu.VMEM((2, 8, 8, rounds) + TILE, jnp.bfloat16),
            pltpu.SemaphoreType.DMA((5,)),
            pltpu.SemaphoreType.DMA((2,)),
            pltpu.SemaphoreType.DMA((3,)),
        ],
        compiler_params=pltpu.CompilerParams(
            collective_id=0, has_side_effects=True, vmem_limit_bytes=32 * 1024 * 1024
        ),
        name="spread_deliver",
    )(
        in_hbm(anchor_features),
        in_hbm(candidate_features),
        in_hbm(anchor_sample_ids.reshape(blocks, rows)),
        in_hbm(candidate_sample_ids.reshape(blocks, rows)),
        in_hbm(opponent_tile),
        sharpness_array,
        score_offset,
    )
    return pl.pallas_call(
        store,
        out_shape=(grad, grad),
        in_specs=[vmem, vmem],
        out_specs=(hbm, hbm),
        scratch_shapes=[pltpu.SemaphoreType.DMA((2,))],
        name="store",
    )(*[pltpu.with_memory_space_constraint(g, pltpu.VMEM) for g in grads])


def solution(mesh):
    placed = (P(("row", "col"), None), P(("row", "col"), None), P(), P(), P(), P(), P())
    return jax.shard_map(
        shards,
        mesh=mesh,
        in_specs=placed,
        out_specs=(P(("row", "col"), None), P(("row", "col"), None)),
        check_vma=False,
    )
```

```python
import random

import jax
import jax.numpy as jnp
from jax import lax
from jax.experimental import pallas as pl
from jax.experimental.pallas import tpu as pltpu
from jax.sharding import PartitionSpec as P

LOGICAL = pl.DeviceIdType.LOGICAL
CHIPS = 4
TILE = (16, 128)


def in_hbm(array):
    return pltpu.with_memory_space_constraint(array, pltpu.HBM)


def in_vmem(array):
    return pltpu.with_memory_space_constraint(array, pltpu.VMEM)


def far_first():
    offsets = [(dx, dy, dz) for dx in range(CHIPS) for dy in range(CHIPS) for dz in range(CHIPS)][1:]
    random.Random(1).shuffle(offsets)
    offsets.sort(key=lambda o: -sum(min(d, CHIPS - d) for d in o))
    return offsets


def block(ref, side, k=None):
    def column(c):
        part = ref[side, :, c] if k is None else ref[side, :, c, k]
        return part.reshape(128, 128)

    return [jnp.concatenate([column(2 * j), column(2 * j + 1)], axis=1) for j in range(4)]


def labels(mine, theirs):
    return jnp.where(mine == theirs, 1.0, -1.0).astype(jnp.float32)


def slope(mine, theirs, label, sharpness, shift):
    score = jnp.zeros((128, 128), jnp.float32)
    for p, q in zip(mine, theirs):
        score += lax.dot_general(p, q, (((1,), (1,)), ((), ())), preferred_element_type=jnp.float32)
    logit = sharpness * score + shift
    return (-sharpness * label * jax.nn.sigmoid(-label * logit)).astype(jnp.bfloat16)


def far_product(mine, theirs, label, sharpness, shift):
    g = jnp.concatenate(
        [slope(mine, t, label[k], sharpness, shift) for k, t in enumerate(theirs)], axis=1
    )
    for j in range(4):
        slab = jnp.concatenate([t[j] for t in theirs], axis=0)
        yield pl.ds(j * 256, 256), jnp.dot(g, slab, preferred_element_type=jnp.float32)


def kernel(
    a_ref,
    b_ref,
    ida_ref,
    idb_ref,
    opponent_hbm,
    sharpness_ref,
    offset_ref,
    grad_a_ref,
    grad_b_ref,
    own,
    far,
    label_ref,
    raw,
    ids,
    opponent_ref,
    mid,
    out,
    load_sem,
    send_sem,
    recv_sem,
):
    rounds = opponent_ref.shape[0]
    loads = [
        pltpu.make_async_copy(src, dst, load_sem.at[i])
        for i, (src, dst) in enumerate(
            (
                (a_ref, raw.at[0]),
                (b_ref, raw.at[1]),
                (ida_ref, ids.at[0]),
                (idb_ref, ids.at[1]),
                (opponent_hbm, opponent_ref),
            )
        )
    ]
    for load in loads:
        load.start()

    row, col = lax.axis_index("row"), lax.axis_index("col")
    x, z_lo = row % CHIPS, row // CHIPS
    y, z_hi, core = col // CHIPS, (col // 2) % 2, col % 2
    z = z_hi * 2 + z_lo
    me = row * 16 + col

    xs = [(x + d) % CHIPS for d in range(CHIPS)]
    ys = [(y + d) % CHIPS for d in range(CHIPS)]
    zs = [(z + d) % CHIPS for d in range(CHIPS)]
    index_x = [v * 16 for v in xs]
    index_y = [v * 4 for v in ys]
    index_z = [(v % 2) * 64 + (v // 2) * 2 for v in zs]
    group_x = [v // 2 for v in xs]
    group_z = [v * 2 for v in zs]
    column_x = [(v % 2) * 4 for v in xs]

    def device(o):
        return index_x[o[0]] + index_y[o[1]] + index_z[o[2]] + o[3]

    def tile_of(o):
        return o[3], group_z[o[2]] + group_x[o[0]], column_x[o[0]] + ys[o[1]]

    chips = far_first()
    here, beside = (0, 0, 0, core), (0, 0, 0, 1 - core)
    spread = [beside] + [o + (c,) for c in range(2) for o in chips]
    deliver = [o + (c,) for c in (1, 0) for o in chips] + [beside]
    barrier = pltpu.get_barrier_semaphore()
    for o in [o + (c,) for o in chips for c in range(2)] + [beside]:
        pl.semaphore_signal(barrier, inc=1, device_id=device(o), device_id_type=LOGICAL)

    for side in range(2):
        loads[side].wait()
        for g in range(8):
            value = raw[side, pl.ds(g * 16, 16), :]
            scale = lax.rsqrt(jnp.sum(value * value, axis=-1, keepdims=True) + 1e-06)
            value = (value * scale).astype(jnp.bfloat16)
            for c in range(8):
                own[side, g, c] = value[:, c * 128 : (c + 1) * 128]

    pl.semaphore_wait(barrier, len(deliver))

    for o in spread:
        pltpu.make_async_remote_copy(
            src_ref=own.at[tile_of(o)],
            dst_ref=mid.at[me],
            send_sem=send_sem.at[0],
            recv_sem=recv_sem.at[0],
            device_id=device(o),
            device_id_type=LOGICAL,
        ).start()
    my_tile = tile_of(here)
    pltpu.make_async_copy(own.at[my_tile], mid.at[me], recv_sem.at[0]).start()

    sharpness = sharpness_ref[0]
    shift = offset_ref[0]

    for load in loads[2:]:
        load.wait()
    grads = (grad_a_ref, grad_b_ref)
    my_ids = []
    for side in range(2):
        line = ids[side, pl.ds(me, 1), :]
        my_ids.append(jnp.transpose(jnp.broadcast_to(line, (128, 128))))
    for side in range(2):
        theirs = block(own, 1 - side)
        label = labels(my_ids[side], ids[1 - side, pl.ds(me, 1), :])
        g = slope(block(own, side), theirs, label, sharpness, shift)
        for j in range(4):
            grads[side][:, j * 256 : (j + 1) * 256] = jnp.dot(g, theirs[j], preferred_element_type=jnp.float32)

    far_label = [
        [labels(my_ids[side], ids[1 - side, pl.ds(opponent_ref[k, me], 1), :]) for k in range(rounds)]
        for side in range(2)
    ]
    for k in range(rounds):
        label_ref[k] = far_label[0][k]

    pltpu.make_async_copy(mid, mid, recv_sem.at[0]).wait()

    def fetch(there):
        for k in range(rounds):
            out[there, k] = mid[opponent_ref[k, there]]

    for o in deliver:
        there = device(o)
        fetch(there)
        pltpu.make_async_remote_copy(
            src_ref=out.at[there],
            dst_ref=far.at[my_tile],
            send_sem=send_sem.at[1],
            recv_sem=recv_sem.at[1 + core],
            device_id=there,
            device_id_type=LOGICAL,
        ).start()
    fetch(me)
    pltpu.make_async_copy(out.at[me], far.at[my_tile], recv_sem.at[1 + core]).start()

    pltpu.make_async_copy(far.at[0], far.at[0], recv_sem.at[1]).wait()
    theirs = [block(far, 0, k) for k in range(rounds)]
    for columns, product in far_product(block(own, 1), theirs, far_label[1], sharpness, shift):
        grad_b_ref[:, columns] += product
    pltpu.make_async_copy(far.at[1], far.at[1], recv_sem.at[2]).wait()

    spread_out = mid.at[pl.ds(0, len(spread))]
    pltpu.make_async_copy(spread_out, spread_out, send_sem.at[0]).wait()
    sent = out.at[pl.ds(0, len(deliver))]
    pltpu.make_async_copy(sent, sent, send_sem.at[1]).wait()


def finish(sharpness_ref, offset_ref, part_a, grad_b, own, far, label_ref, out_a, out_b, total, sem):
    copies = [pltpu.make_async_copy(grad_b, out_b, sem.at[4])]
    copies[0].start()
    rounds = label_ref.shape[0]
    theirs = [block(far, 1, k) for k in range(rounds)]
    label = [label_ref[k] for k in range(rounds)]
    for j, (columns, product) in enumerate(
        far_product(block(own, 0), theirs, label, sharpness_ref[0], offset_ref[0])
    ):
        total[:, columns] = part_a[:, columns] + product
        copies.append(pltpu.make_async_copy(total.at[:, columns], out_a.at[:, columns], sem.at[j]))
        copies[-1].start()
    for copy in copies:
        copy.wait()


def shards(
    anchor_features,
    candidate_features,
    anchor_sample_ids,
    candidate_sample_ids,
    opponent_tile,
    sharpness_array,
    score_offset,
):
    rows, width = anchor_features.shape
    rounds, blocks = opponent_tile.shape
    hbm = pl.BlockSpec(memory_space=pltpu.HBM)
    vmem = pl.BlockSpec(memory_space=pltpu.VMEM)
    smem = pl.BlockSpec(memory_space=pltpu.SMEM)
    grad = jax.ShapeDtypeStruct((rows, width), jnp.float32)
    parts = pl.pallas_call(
        kernel,
        out_shape=(
            grad,
            grad,
            jax.ShapeDtypeStruct((2, 8, 8) + TILE, jnp.bfloat16),
            jax.ShapeDtypeStruct((2, 8, 8, rounds) + TILE, jnp.bfloat16),
            jax.ShapeDtypeStruct((rounds, rows, rows), jnp.float32),
        ),
        in_specs=[hbm, hbm, hbm, hbm, hbm, smem, smem],
        out_specs=(vmem,) * 5,
        scratch_shapes=[
            pltpu.VMEM((2, rows, width), jnp.float32),
            pltpu.VMEM((2, blocks, rows), jnp.int32),
            pltpu.SMEM((rounds, blocks), jnp.int32),
            pltpu.VMEM((blocks,) + TILE, jnp.bfloat16),
            pltpu.VMEM((blocks, rounds) + TILE, jnp.bfloat16),
            pltpu.SemaphoreType.DMA((5,)),
            pltpu.SemaphoreType.DMA((2,)),
            pltpu.SemaphoreType.DMA((3,)),
        ],
        compiler_params=pltpu.CompilerParams(
            collective_id=0, has_side_effects=True, vmem_limit_bytes=32 * 1024 * 1024
        ),
        name="spread_deliver",
    )(
        in_hbm(anchor_features),
        in_hbm(candidate_features),
        in_hbm(anchor_sample_ids.reshape(blocks, rows)),
        in_hbm(candidate_sample_ids.reshape(blocks, rows)),
        in_hbm(opponent_tile),
        sharpness_array,
        score_offset,
    )
    return pl.pallas_call(
        finish,
        out_shape=(grad, grad),
        in_specs=[smem, smem] + [vmem] * 5,
        out_specs=(hbm, hbm),
        scratch_shapes=[pltpu.VMEM((rows, width), jnp.float32), pltpu.SemaphoreType.DMA((5,))],
        compiler_params=pltpu.CompilerParams(vmem_limit_bytes=16 * 1024 * 1024),
        name="finish",
    )(sharpness_array, score_offset, *[in_vmem(p) for p in parts])


def solution(mesh):
    placed = (P(("row", "col"), None), P(("row", "col"), None), P(), P(), P(), P(), P())
    return jax.shard_map(
        shards,
        mesh=mesh,
        in_specs=placed,
        out_specs=(P(("row", "col"), None), P(("row", "col"), None)),
        check_vma=False,
    )
```

```python
import random

import jax
import jax.numpy as jnp
from jax import lax
from jax.experimental import pallas as pl
from jax.experimental.pallas import tpu as pltpu
from jax.sharding import PartitionSpec as P

LOGICAL = pl.DeviceIdType.LOGICAL
CHIPS = 4
TILE = (16, 128)


def in_hbm(array):
    return pltpu.with_memory_space_constraint(array, pltpu.HBM)


def in_vmem(array):
    return pltpu.with_memory_space_constraint(array, pltpu.VMEM)


def far_first():
    offsets = [(dx, dy, dz) for dx in range(CHIPS) for dy in range(CHIPS) for dz in range(CHIPS)][1:]
    random.Random(4).shuffle(offsets)
    offsets.sort(key=lambda o: -sum(min(d, CHIPS - d) for d in o))
    return offsets


def block(ref, side, k=None):
    def column(c):
        part = ref[side, :, c] if k is None else ref[side, :, c, k]
        return part.reshape(128, 128)

    return [jnp.concatenate([column(2 * j), column(2 * j + 1)], axis=1) for j in range(4)]


def labels(mine, theirs):
    return jnp.where(mine == theirs, 1.0, -1.0).astype(jnp.float32)


def slope(mine, theirs, label, sharpness, shift):
    score = jnp.zeros((128, 128), jnp.float32)
    for p, q in zip(mine, theirs):
        score += lax.dot_general(p, q, (((1,), (1,)), ((), ())), preferred_element_type=jnp.float32)
    logit = sharpness * score + shift
    return (-sharpness * label * jax.nn.sigmoid(-label * logit)).astype(jnp.bfloat16)


def far_product(mine, theirs, label, sharpness, shift):
    g = jnp.concatenate(
        [slope(mine, t, label[k], sharpness, shift) for k, t in enumerate(theirs)], axis=1
    )
    for j in range(4):
        slab = jnp.concatenate([t[j] for t in theirs], axis=0)
        yield pl.ds(j * 256, 256), jnp.dot(g, slab, preferred_element_type=jnp.float32)


def kernel(
    a_ref,
    b_ref,
    ida_ref,
    idb_ref,
    opponent_hbm,
    sharpness_ref,
    offset_ref,
    grad_a_ref,
    grad_b_ref,
    own,
    far,
    label_ref,
    raw,
    ids,
    opponent_ref,
    mid,
    out,
    load_sem,
    send_sem,
    recv_sem,
):
    rounds = opponent_ref.shape[0]
    loads = [
        pltpu.make_async_copy(src, dst, load_sem.at[i])
        for i, (src, dst) in enumerate(
            (
                (a_ref, raw.at[0]),
                (b_ref, raw.at[1]),
                (ida_ref, ids.at[0]),
                (idb_ref, ids.at[1]),
                (opponent_hbm, opponent_ref),
            )
        )
    ]
    for load in loads:
        load.start()

    row, col = lax.axis_index("row"), lax.axis_index("col")
    x, z_lo = row % CHIPS, row // CHIPS
    y, z_hi, core = col // CHIPS, (col // 2) % 2, col % 2
    z = z_hi * 2 + z_lo
    me = row * 16 + col

    xs = [(x + d) % CHIPS for d in range(CHIPS)]
    ys = [(y + d) % CHIPS for d in range(CHIPS)]
    zs = [(z + d) % CHIPS for d in range(CHIPS)]
    index_x = [v * 16 for v in xs]
    index_y = [v * 4 for v in ys]
    index_z = [(v % 2) * 64 + (v // 2) * 2 for v in zs]
    group_x = [v // 2 for v in xs]
    group_z = [v * 2 for v in zs]
    column_x = [(v % 2) * 4 for v in xs]

    def device(o):
        return index_x[o[0]] + index_y[o[1]] + index_z[o[2]] + o[3]

    def tile_of(o):
        return o[3], group_z[o[2]] + group_x[o[0]], column_x[o[0]] + ys[o[1]]

    chips = far_first()
    here, beside = (0, 0, 0, core), (0, 0, 0, 1 - core)
    spread = [beside] + [o + (c,) for c in range(2) for o in chips]
    deliver = [o + (c,) for c in (1, 0) for o in chips] + [beside]
    barrier = pltpu.get_barrier_semaphore()
    for o in [o + (c,) for o in chips for c in range(2)] + [beside]:
        pl.semaphore_signal(barrier, inc=1, device_id=device(o), device_id_type=LOGICAL)

    for side in range(2):
        loads[side].wait()
        for g in range(8):
            value = raw[side, pl.ds(g * 16, 16), :]
            scale = lax.rsqrt(jnp.sum(value * value, axis=-1, keepdims=True) + 1e-06)
            value = (value * scale).astype(jnp.bfloat16)
            for c in range(8):
                own[side, g, c] = value[:, c * 128 : (c + 1) * 128]

    pl.semaphore_wait(barrier, len(deliver))

    for o in spread:
        pltpu.make_async_remote_copy(
            src_ref=own.at[tile_of(o)],
            dst_ref=mid.at[me],
            send_sem=send_sem.at[0],
            recv_sem=recv_sem.at[0],
            device_id=device(o),
            device_id_type=LOGICAL,
        ).start()
    my_tile = tile_of(here)
    pltpu.make_async_copy(own.at[my_tile], mid.at[me], recv_sem.at[0]).start()

    sharpness = sharpness_ref[0]
    shift = offset_ref[0]

    for load in loads[2:]:
        load.wait()
    grads = (grad_a_ref, grad_b_ref)
    my_ids = []
    for side in range(2):
        line = ids[side, pl.ds(me, 1), :]
        my_ids.append(jnp.transpose(jnp.broadcast_to(line, (128, 128))))
    for side in range(2):
        theirs = block(own, 1 - side)
        label = labels(my_ids[side], ids[1 - side, pl.ds(me, 1), :])
        g = slope(block(own, side), theirs, label, sharpness, shift)
        for j in range(4):
            grads[side][:, j * 256 : (j + 1) * 256] = jnp.dot(g, theirs[j], preferred_element_type=jnp.float32)

    far_label = [
        [labels(my_ids[side], ids[1 - side, pl.ds(opponent_ref[k, me], 1), :]) for k in range(rounds)]
        for side in range(2)
    ]
    for k in range(rounds):
        label_ref[k] = far_label[0][k]

    pltpu.make_async_copy(mid, mid, recv_sem.at[0]).wait()

    def fetch(there):
        for k in range(rounds):
            out[there, k] = mid[opponent_ref[k, there]]

    for o in deliver:
        there = device(o)
        fetch(there)
        pltpu.make_async_remote_copy(
            src_ref=out.at[there],
            dst_ref=far.at[my_tile],
            send_sem=send_sem.at[1],
            recv_sem=recv_sem.at[1 + core],
            device_id=there,
            device_id_type=LOGICAL,
        ).start()
    fetch(me)
    pltpu.make_async_copy(out.at[me], far.at[my_tile], recv_sem.at[1 + core]).start()

    pltpu.make_async_copy(far.at[0], far.at[0], recv_sem.at[1]).wait()
    theirs = [block(far, 0, k) for k in range(rounds)]
    for columns, product in far_product(block(own, 1), theirs, far_label[1], sharpness, shift):
        grad_b_ref[:, columns] += product
    pltpu.make_async_copy(far.at[1], far.at[1], recv_sem.at[2]).wait()

    spread_out = mid.at[pl.ds(0, len(spread))]
    pltpu.make_async_copy(spread_out, spread_out, send_sem.at[0]).wait()
    sent = out.at[pl.ds(0, len(deliver))]
    pltpu.make_async_copy(sent, sent, send_sem.at[1]).wait()


def finish(sharpness_ref, offset_ref, part_a, grad_b, own, far, label_ref, out_a, out_b, total, sem):
    copies = [pltpu.make_async_copy(grad_b, out_b, sem.at[4])]
    copies[0].start()
    rounds = label_ref.shape[0]
    theirs = [block(far, 1, k) for k in range(rounds)]
    label = [label_ref[k] for k in range(rounds)]
    for j, (columns, product) in enumerate(
        far_product(block(own, 0), theirs, label, sharpness_ref[0], offset_ref[0])
    ):
        total[:, columns] = part_a[:, columns] + product
        copies.append(pltpu.make_async_copy(total.at[:, columns], out_a.at[:, columns], sem.at[j]))
        copies[-1].start()
    for copy in copies:
        copy.wait()


def shards(
    anchor_features,
    candidate_features,
    anchor_sample_ids,
    candidate_sample_ids,
    opponent_tile,
    sharpness_array,
    score_offset,
):
    rows, width = anchor_features.shape
    rounds, blocks = opponent_tile.shape
    hbm = pl.BlockSpec(memory_space=pltpu.HBM)
    vmem = pl.BlockSpec(memory_space=pltpu.VMEM)
    smem = pl.BlockSpec(memory_space=pltpu.SMEM)
    grad = jax.ShapeDtypeStruct((rows, width), jnp.float32)
    parts = pl.pallas_call(
        kernel,
        out_shape=(
            grad,
            grad,
            jax.ShapeDtypeStruct((2, 8, 8) + TILE, jnp.bfloat16),
            jax.ShapeDtypeStruct((2, 8, 8, rounds) + TILE, jnp.bfloat16),
            jax.ShapeDtypeStruct((rounds, rows, rows), jnp.float32),
        ),
        in_specs=[hbm, hbm, hbm, hbm, hbm, smem, smem],
        out_specs=(vmem,) * 5,
        scratch_shapes=[
            pltpu.VMEM((2, rows, width), jnp.float32),
            pltpu.VMEM((2, blocks, rows), jnp.int32),
            pltpu.SMEM((rounds, blocks), jnp.int32),
            pltpu.VMEM((blocks,) + TILE, jnp.bfloat16),
            pltpu.VMEM((blocks, rounds) + TILE, jnp.bfloat16),
            pltpu.SemaphoreType.DMA((5,)),
            pltpu.SemaphoreType.DMA((2,)),
            pltpu.SemaphoreType.DMA((3,)),
        ],
        compiler_params=pltpu.CompilerParams(
            collective_id=0, has_side_effects=True, vmem_limit_bytes=32 * 1024 * 1024
        ),
        name="spread_deliver",
    )(
        in_hbm(anchor_features),
        in_hbm(candidate_features),
        in_hbm(anchor_sample_ids.reshape(blocks, rows)),
        in_hbm(candidate_sample_ids.reshape(blocks, rows)),
        in_hbm(opponent_tile),
        sharpness_array,
        score_offset,
    )
    return pl.pallas_call(
        finish,
        out_shape=(grad, grad),
        in_specs=[smem, smem] + [vmem] * 5,
        out_specs=(hbm, hbm),
        scratch_shapes=[pltpu.VMEM((rows, width), jnp.float32), pltpu.SemaphoreType.DMA((5,))],
        compiler_params=pltpu.CompilerParams(vmem_limit_bytes=16 * 1024 * 1024),
        name="finish",
    )(sharpness_array, score_offset, *[in_vmem(p) for p in parts])


def solution(mesh):
    placed = (P(("row", "col"), None), P(("row", "col"), None), P(), P(), P(), P(), P())
    return jax.shard_map(
        shards,
        mesh=mesh,
        in_specs=placed,
        out_specs=(P(("row", "col"), None), P(("row", "col"), None)),
        check_vma=False,
    )
```

```python
import random

import jax
import jax.numpy as jnp
from jax import lax
from jax.experimental import pallas as pl
from jax.experimental.pallas import tpu as pltpu
from jax.sharding import PartitionSpec as P

LOGICAL = pl.DeviceIdType.LOGICAL
CHIPS = 4
TILE = (16, 128)


def in_hbm(array):
    return pltpu.with_memory_space_constraint(array, pltpu.HBM)


def in_vmem(array):
    return pltpu.with_memory_space_constraint(array, pltpu.VMEM)


def far_first():
    offsets = [(dx, dy, dz) for dx in range(CHIPS) for dy in range(CHIPS) for dz in range(CHIPS)][1:]
    random.Random(4).shuffle(offsets)
    offsets.sort(key=lambda o: -sum(min(d, CHIPS - d) for d in o))
    return offsets


def block(ref, side, k=None):
    def column(c):
        part = ref[side, :, c] if k is None else ref[side, :, c, k]
        return part.reshape(128, 128)

    return [jnp.concatenate([column(2 * j), column(2 * j + 1)], axis=1) for j in range(4)]


def labels(mine, theirs):
    return jnp.where(mine == theirs, 1.0, -1.0).astype(jnp.float32)


def slope(mine, theirs, label, sharpness, shift):
    score = jnp.zeros((128, 128), jnp.float32)
    for p, q in zip(mine, theirs):
        score += lax.dot_general(p, q, (((1,), (1,)), ((), ())), preferred_element_type=jnp.float32)
    logit = sharpness * score + shift
    return (-sharpness * label * jax.nn.sigmoid(-label * logit)).astype(jnp.bfloat16)


def far_product(mine, theirs, label, sharpness, shift):
    g = jnp.concatenate(
        [slope(mine, t, label[k], sharpness, shift) for k, t in enumerate(theirs)], axis=1
    )
    for j in range(4):
        slab = jnp.concatenate([t[j] for t in theirs], axis=0)
        yield pl.ds(j * 256, 256), jnp.dot(g, slab, preferred_element_type=jnp.float32)


def kernel(
    a_ref,
    b_ref,
    ida_ref,
    idb_ref,
    opponent_hbm,
    sharpness_ref,
    offset_ref,
    grad_a_ref,
    grad_b_ref,
    own,
    far,
    label_ref,
    raw,
    ids,
    opponent_ref,
    mid,
    out,
    load_sem,
    send_sem,
    recv_sem,
):
    rounds = opponent_ref.shape[0]
    loads = [
        pltpu.make_async_copy(src, dst, load_sem.at[i])
        for i, (src, dst) in enumerate(
            (
                (a_ref, raw.at[0]),
                (b_ref, raw.at[1]),
                (ida_ref, ids.at[0]),
                (idb_ref, ids.at[1]),
                (opponent_hbm, opponent_ref),
            )
        )
    ]
    for load in loads:
        load.start()

    row, col = lax.axis_index("row"), lax.axis_index("col")
    x, z_lo = row % CHIPS, row // CHIPS
    y, z_hi, core = col // CHIPS, (col // 2) % 2, col % 2
    z = z_hi * 2 + z_lo
    me = row * 16 + col

    xs = [(x + d) % CHIPS for d in range(CHIPS)]
    ys = [(y + d) % CHIPS for d in range(CHIPS)]
    zs = [(z + d) % CHIPS for d in range(CHIPS)]
    index_x = [v * 16 for v in xs]
    index_y = [v * 4 for v in ys]
    index_z = [(v % 2) * 64 + (v // 2) * 2 for v in zs]
    group_x = [v // 2 for v in xs]
    group_z = [v * 2 for v in zs]
    column_x = [(v % 2) * 4 for v in xs]

    def device(o):
        return index_x[o[0]] + index_y[o[1]] + index_z[o[2]] + o[3]

    def tile_of(o):
        return o[3], group_z[o[2]] + group_x[o[0]], column_x[o[0]] + ys[o[1]]

    chips = far_first()
    here, beside = (0, 0, 0, core), (0, 0, 0, 1 - core)
    spread = [beside] + [o + (c,) for c in range(2) for o in chips]
    deliver = [o + (c,) for _, c, o in sorted([(i + 36 * (c != 1), c, o) for i, o in enumerate(chips) for c in range(2)])] + [beside]
    barrier = pltpu.get_barrier_semaphore()
    for o in [o + (c,) for o in chips for c in range(2)] + [beside]:
        pl.semaphore_signal(barrier, inc=1, device_id=device(o), device_id_type=LOGICAL)

    for side in range(2):
        loads[side].wait()
        for g in range(8):
            value = raw[side, pl.ds(g * 16, 16), :]
            scale = lax.rsqrt(jnp.sum(value * value, axis=-1, keepdims=True) + 1e-06)
            value = (value * scale).astype(jnp.bfloat16)
            for c in range(8):
                own[side, g, c] = value[:, c * 128 : (c + 1) * 128]

    pl.semaphore_wait(barrier, len(deliver))

    for o in spread:
        pltpu.make_async_remote_copy(
            src_ref=own.at[tile_of(o)],
            dst_ref=mid.at[me],
            send_sem=send_sem.at[0],
            recv_sem=recv_sem.at[0],
            device_id=device(o),
            device_id_type=LOGICAL,
        ).start()
    my_tile = tile_of(here)
    pltpu.make_async_copy(own.at[my_tile], mid.at[me], recv_sem.at[0]).start()

    sharpness = sharpness_ref[0]
    shift = offset_ref[0]

    for load in loads[2:]:
        load.wait()
    grads = (grad_a_ref, grad_b_ref)
    my_ids = []
    for side in range(2):
        line = ids[side, pl.ds(me, 1), :]
        my_ids.append(jnp.transpose(jnp.broadcast_to(line, (128, 128))))
    pltpu.make_async_copy(mid, mid, recv_sem.at[0]).wait()

    def fetch(there):
        for k in range(rounds):
            out[there, k] = mid[opponent_ref[k, there]]

    for o in deliver:
        there = device(o)
        fetch(there)
        pltpu.make_async_remote_copy(
            src_ref=out.at[there],
            dst_ref=far.at[my_tile],
            send_sem=send_sem.at[1],
            recv_sem=recv_sem.at[1 + core],
            device_id=there,
            device_id_type=LOGICAL,
        ).start()
    fetch(me)
    pltpu.make_async_copy(out.at[me], far.at[my_tile], recv_sem.at[1 + core]).start()

    far_label = [
        [labels(my_ids[side], ids[1 - side, pl.ds(opponent_ref[k, me], 1), :]) for k in range(rounds)]
        for side in range(2)
    ]
    for k in range(rounds):
        label_ref[k] = far_label[0][k]


    for side in range(2):
        theirs = block(own, 1 - side)
        label = labels(my_ids[side], ids[1 - side, pl.ds(me, 1), :])
        g = slope(block(own, side), theirs, label, sharpness, shift)
        for j in range(4):
            grads[side][:, j * 256 : (j + 1) * 256] = jnp.dot(g, theirs[j], preferred_element_type=jnp.float32)


    pltpu.make_async_copy(far.at[0], far.at[0], recv_sem.at[1]).wait()
    theirs = [block(far, 0, k) for k in range(rounds)]
    for columns, product in far_product(block(own, 1), theirs, far_label[1], sharpness, shift):
        grad_b_ref[:, columns] += product
    pltpu.make_async_copy(far.at[1], far.at[1], recv_sem.at[2]).wait()

    spread_out = mid.at[pl.ds(0, len(spread))]
    pltpu.make_async_copy(spread_out, spread_out, send_sem.at[0]).wait()
    sent = out.at[pl.ds(0, len(deliver))]
    pltpu.make_async_copy(sent, sent, send_sem.at[1]).wait()


def finish(sharpness_ref, offset_ref, part_a, grad_b, own, far, label_ref, out_a, out_b, total, sem):
    copies = [pltpu.make_async_copy(grad_b, out_b, sem.at[4])]
    copies[0].start()
    rounds = label_ref.shape[0]
    theirs = [block(far, 1, k) for k in range(rounds)]
    label = [label_ref[k] for k in range(rounds)]
    for j, (columns, product) in enumerate(
        far_product(block(own, 0), theirs, label, sharpness_ref[0], offset_ref[0])
    ):
        total[:, columns] = part_a[:, columns] + product
        copies.append(pltpu.make_async_copy(total.at[:, columns], out_a.at[:, columns], sem.at[j]))
        copies[-1].start()
    for copy in copies:
        copy.wait()


def shards(
    anchor_features,
    candidate_features,
    anchor_sample_ids,
    candidate_sample_ids,
    opponent_tile,
    sharpness_array,
    score_offset,
):
    rows, width = anchor_features.shape
    rounds, blocks = opponent_tile.shape
    hbm = pl.BlockSpec(memory_space=pltpu.HBM)
    vmem = pl.BlockSpec(memory_space=pltpu.VMEM)
    smem = pl.BlockSpec(memory_space=pltpu.SMEM)
    grad = jax.ShapeDtypeStruct((rows, width), jnp.float32)
    parts = pl.pallas_call(
        kernel,
        out_shape=(
            grad,
            grad,
            jax.ShapeDtypeStruct((2, 8, 8) + TILE, jnp.bfloat16),
            jax.ShapeDtypeStruct((2, 8, 8, rounds) + TILE, jnp.bfloat16),
            jax.ShapeDtypeStruct((rounds, rows, rows), jnp.float32),
        ),
        in_specs=[hbm, hbm, hbm, hbm, hbm, smem, smem],
        out_specs=(vmem,) * 5,
        scratch_shapes=[
            pltpu.VMEM((2, rows, width), jnp.float32),
            pltpu.VMEM((2, blocks, rows), jnp.int32),
            pltpu.SMEM((rounds, blocks), jnp.int32),
            pltpu.VMEM((blocks,) + TILE, jnp.bfloat16),
            pltpu.VMEM((blocks, rounds) + TILE, jnp.bfloat16),
            pltpu.SemaphoreType.DMA((5,)),
            pltpu.SemaphoreType.DMA((2,)),
            pltpu.SemaphoreType.DMA((3,)),
        ],
        compiler_params=pltpu.CompilerParams(
            collective_id=0, has_side_effects=True, vmem_limit_bytes=32 * 1024 * 1024
        ),
        name="spread_deliver",
    )(
        in_hbm(anchor_features),
        in_hbm(candidate_features),
        in_hbm(anchor_sample_ids.reshape(blocks, rows)),
        in_hbm(candidate_sample_ids.reshape(blocks, rows)),
        in_hbm(opponent_tile),
        sharpness_array,
        score_offset,
    )
    return pl.pallas_call(
        finish,
        out_shape=(grad, grad),
        in_specs=[smem, smem] + [vmem] * 5,
        out_specs=(hbm, hbm),
        scratch_shapes=[pltpu.VMEM((rows, width), jnp.float32), pltpu.SemaphoreType.DMA((5,))],
        compiler_params=pltpu.CompilerParams(vmem_limit_bytes=16 * 1024 * 1024),
        name="finish",
    )(sharpness_array, score_offset, *[in_vmem(p) for p in parts])


def solution(mesh):
    placed = (P(("row", "col"), None), P(("row", "col"), None), P(), P(), P(), P(), P())
    return jax.shard_map(
        shards,
        mesh=mesh,
        in_specs=placed,
        out_specs=(P(("row", "col"), None), P(("row", "col"), None)),
        check_vma=False,
    )
```

```python
import random

import jax
import jax.numpy as jnp
from jax import lax
from jax.experimental import pallas as pl
from jax.experimental.pallas import tpu as pltpu
from jax.sharding import PartitionSpec as P

LOGICAL = pl.DeviceIdType.LOGICAL
CHIPS = 4
TILE = (16, 128)


def in_hbm(array):
    return pltpu.with_memory_space_constraint(array, pltpu.HBM)


def in_vmem(array):
    return pltpu.with_memory_space_constraint(array, pltpu.VMEM)


def far_first():
    offsets = [(dx, dy, dz) for dx in range(CHIPS) for dy in range(CHIPS) for dz in range(CHIPS)][1:]
    random.Random(4).shuffle(offsets)
    offsets.sort(key=lambda o: -sum(min(d, CHIPS - d) for d in o))
    return offsets


def block(ref, side, k=None):
    def column(c):
        part = ref[side, :, c] if k is None else ref[side, :, c, k]
        return part.reshape(128, 128)

    return [jnp.concatenate([column(2 * j), column(2 * j + 1)], axis=1) for j in range(4)]


def labels(mine, theirs):
    return jnp.where(mine == theirs, 1.0, -1.0).astype(jnp.float32)


def slope(mine, theirs, label, sharpness, shift):
    score = jnp.zeros((128, 128), jnp.float32)
    for p, q in zip(mine, theirs):
        score += lax.dot_general(p, q, (((1,), (1,)), ((), ())), preferred_element_type=jnp.float32)
    logit = sharpness * score + shift
    return (-sharpness * label * jax.nn.sigmoid(-label * logit)).astype(jnp.bfloat16)


def far_product(mine, theirs, label, sharpness, shift):
    g = jnp.concatenate(
        [slope(mine, t, label[k], sharpness, shift) for k, t in enumerate(theirs)], axis=1
    )
    for j in range(4):
        slab = jnp.concatenate([t[j] for t in theirs], axis=0)
        yield pl.ds(j * 256, 256), jnp.dot(g, slab, preferred_element_type=jnp.float32)


def kernel(
    a_ref,
    b_ref,
    ida_ref,
    idb_ref,
    opponent_hbm,
    sharpness_ref,
    offset_ref,
    grad_a_ref,
    grad_b_ref,
    own,
    far,
    label_ref,
    raw,
    ids,
    opponent_ref,
    mid,
    out,
    load_sem,
    send_sem,
    recv_sem,
    entered,
):
    rounds = opponent_ref.shape[0]
    loads = [
        pltpu.make_async_copy(src, dst, load_sem.at[i])
        for i, (src, dst) in enumerate(
            (
                (a_ref, raw.at[0]),
                (b_ref, raw.at[1]),
                (ida_ref, ids.at[0]),
                (idb_ref, ids.at[1]),
                (opponent_hbm, opponent_ref),
            )
        )
    ]
    for load in loads:
        load.start()

    row, col = lax.axis_index("row"), lax.axis_index("col")
    x, z_lo = row % CHIPS, row // CHIPS
    y, z_hi, core = col // CHIPS, (col // 2) % 2, col % 2
    z = z_hi * 2 + z_lo
    me = row * 16 + col

    xs = [(x + d) % CHIPS for d in range(CHIPS)]
    ys = [(y + d) % CHIPS for d in range(CHIPS)]
    zs = [(z + d) % CHIPS for d in range(CHIPS)]
    index_x = [v * 16 for v in xs]
    index_y = [v * 4 for v in ys]
    index_z = [(v % 2) * 64 + (v // 2) * 2 for v in zs]
    group_x = [v // 2 for v in xs]
    group_z = [v * 2 for v in zs]
    column_x = [(v % 2) * 4 for v in xs]

    def device(o):
        return index_x[o[0]] + index_y[o[1]] + index_z[o[2]] + o[3]

    def tile_of(o):
        return o[3], group_z[o[2]] + group_x[o[0]], column_x[o[0]] + ys[o[1]]

    chips = far_first()
    here, beside = (0, 0, 0, core), (0, 0, 0, 1 - core)
    spread = [[o + (c,) for o in chips] for c in range(2)]
    spread[1].append(beside)
    deliver = [o + (c,) for c in (1, 0) for o in chips] + [beside]
    barrier = pltpu.get_barrier_semaphore()
    greeted = [o + (core,) for o in chips] + [beside]
    for o in greeted:
        pl.semaphore_signal(barrier, inc=1, device_id=device(o), device_id_type=LOGICAL)

    for side in range(2):
        loads[side].wait()
        for g in range(8):
            value = raw[side, pl.ds(g * 16, 16), :]
            scale = lax.rsqrt(jnp.sum(value * value, axis=-1, keepdims=True) + 1e-06)
            value = (value * scale).astype(jnp.bfloat16)
            for c in range(8):
                own[side, g, c] = value[:, c * 128 : (c + 1) * 128]

    pl.semaphore_wait(barrier, len(greeted))
    pl.semaphore_signal(entered, inc=1, device_id=device(beside), device_id_type=LOGICAL)

    for c in range(2):
        @pl.when(core != c)
        def _():
            pl.semaphore_wait(entered, 1)
        for o in spread[c]:
            pltpu.make_async_remote_copy(
                src_ref=own.at[tile_of(o)],
                dst_ref=mid.at[me],
                send_sem=send_sem.at[0],
                recv_sem=recv_sem.at[0],
                device_id=device(o),
                device_id_type=LOGICAL,
            ).start()
    my_tile = tile_of(here)
    pltpu.make_async_copy(own.at[my_tile], mid.at[me], recv_sem.at[0]).start()

    sharpness = sharpness_ref[0]
    shift = offset_ref[0]

    for load in loads[2:]:
        load.wait()
    grads = (grad_a_ref, grad_b_ref)
    my_ids = []
    for side in range(2):
        line = ids[side, pl.ds(me, 1), :]
        my_ids.append(jnp.transpose(jnp.broadcast_to(line, (128, 128))))
    for side in range(2):
        theirs = block(own, 1 - side)
        label = labels(my_ids[side], ids[1 - side, pl.ds(me, 1), :])
        g = slope(block(own, side), theirs, label, sharpness, shift)
        for j in range(4):
            grads[side][:, j * 256 : (j + 1) * 256] = jnp.dot(g, theirs[j], preferred_element_type=jnp.float32)

    far_label = [
        [labels(my_ids[side], ids[1 - side, pl.ds(opponent_ref[k, me], 1), :]) for k in range(rounds)]
        for side in range(2)
    ]
    for k in range(rounds):
        label_ref[k] = far_label[0][k]

    pltpu.make_async_copy(mid, mid, recv_sem.at[0]).wait()

    def fetch(there):
        for k in range(rounds):
            out[there, k] = mid[opponent_ref[k, there]]

    for o in deliver:
        there = device(o)
        fetch(there)
        pltpu.make_async_remote_copy(
            src_ref=out.at[there],
            dst_ref=far.at[my_tile],
            send_sem=send_sem.at[1],
            recv_sem=recv_sem.at[1 + core],
            device_id=there,
            device_id_type=LOGICAL,
        ).start()
    fetch(me)
    pltpu.make_async_copy(out.at[me], far.at[my_tile], recv_sem.at[1 + core]).start()

    pltpu.make_async_copy(far.at[0], far.at[0], recv_sem.at[1]).wait()
    theirs = [block(far, 0, k) for k in range(rounds)]
    for columns, product in far_product(block(own, 1), theirs, far_label[1], sharpness, shift):
        grad_b_ref[:, columns] += product
    pltpu.make_async_copy(far.at[1], far.at[1], recv_sem.at[2]).wait()

    spread_out = mid.at[pl.ds(0, len(deliver))]
    pltpu.make_async_copy(spread_out, spread_out, send_sem.at[0]).wait()
    sent = out.at[pl.ds(0, len(deliver))]
    pltpu.make_async_copy(sent, sent, send_sem.at[1]).wait()


def finish(sharpness_ref, offset_ref, part_a, grad_b, own, far, label_ref, out_a, out_b, total, sem):
    copies = [pltpu.make_async_copy(grad_b, out_b, sem.at[4])]
    copies[0].start()
    rounds = label_ref.shape[0]
    theirs = [block(far, 1, k) for k in range(rounds)]
    label = [label_ref[k] for k in range(rounds)]
    for j, (columns, product) in enumerate(
        far_product(block(own, 0), theirs, label, sharpness_ref[0], offset_ref[0])
    ):
        total[:, columns] = part_a[:, columns] + product
        copies.append(pltpu.make_async_copy(total.at[:, columns], out_a.at[:, columns], sem.at[j]))
        copies[-1].start()
    for copy in copies:
        copy.wait()


def shards(
    anchor_features,
    candidate_features,
    anchor_sample_ids,
    candidate_sample_ids,
    opponent_tile,
    sharpness_array,
    score_offset,
):
    rows, width = anchor_features.shape
    rounds, blocks = opponent_tile.shape
    hbm = pl.BlockSpec(memory_space=pltpu.HBM)
    vmem = pl.BlockSpec(memory_space=pltpu.VMEM)
    smem = pl.BlockSpec(memory_space=pltpu.SMEM)
    grad = jax.ShapeDtypeStruct((rows, width), jnp.float32)
    parts = pl.pallas_call(
        kernel,
        out_shape=(
            grad,
            grad,
            jax.ShapeDtypeStruct((2, 8, 8) + TILE, jnp.bfloat16),
            jax.ShapeDtypeStruct((2, 8, 8, rounds) + TILE, jnp.bfloat16),
            jax.ShapeDtypeStruct((rounds, rows, rows), jnp.float32),
        ),
        in_specs=[hbm, hbm, hbm, hbm, hbm, smem, smem],
        out_specs=(vmem,) * 5,
        scratch_shapes=[
            pltpu.VMEM((2, rows, width), jnp.float32),
            pltpu.VMEM((2, blocks, rows), jnp.int32),
            pltpu.SMEM((rounds, blocks), jnp.int32),
            pltpu.VMEM((blocks,) + TILE, jnp.bfloat16),
            pltpu.VMEM((blocks, rounds) + TILE, jnp.bfloat16),
            pltpu.SemaphoreType.DMA((5,)),
            pltpu.SemaphoreType.DMA((2,)),
            pltpu.SemaphoreType.DMA((3,)),
            pltpu.SemaphoreType.REGULAR,
        ],
        compiler_params=pltpu.CompilerParams(
            collective_id=0, has_side_effects=True, vmem_limit_bytes=32 * 1024 * 1024
        ),
        name="spread_deliver",
    )(
        in_hbm(anchor_features),
        in_hbm(candidate_features),
        in_hbm(anchor_sample_ids.reshape(blocks, rows)),
        in_hbm(candidate_sample_ids.reshape(blocks, rows)),
        in_hbm(opponent_tile),
        sharpness_array,
        score_offset,
    )
    return pl.pallas_call(
        finish,
        out_shape=(grad, grad),
        in_specs=[smem, smem] + [vmem] * 5,
        out_specs=(hbm, hbm),
        scratch_shapes=[pltpu.VMEM((rows, width), jnp.float32), pltpu.SemaphoreType.DMA((5,))],
        compiler_params=pltpu.CompilerParams(vmem_limit_bytes=16 * 1024 * 1024),
        name="finish",
    )(sharpness_array, score_offset, *[in_vmem(p) for p in parts])


def solution(mesh):
    placed = (P(("row", "col"), None), P(("row", "col"), None), P(), P(), P(), P(), P())
    return jax.shard_map(
        shards,
        mesh=mesh,
        in_specs=placed,
        out_specs=(P(("row", "col"), None), P(("row", "col"), None)),
        check_vma=False,
    )
```

```python
import random

import jax
import jax.numpy as jnp
from jax import lax
from jax.experimental import pallas as pl
from jax.experimental.pallas import tpu as pltpu
from jax.sharding import PartitionSpec as P

LOGICAL = pl.DeviceIdType.LOGICAL
CHIPS = 4
TILE = (16, 128)


def in_hbm(array):
    return pltpu.with_memory_space_constraint(array, pltpu.HBM)


def in_vmem(array):
    return pltpu.with_memory_space_constraint(array, pltpu.VMEM)


def far_first():
    offsets = [(dx, dy, dz) for dx in range(CHIPS) for dy in range(CHIPS) for dz in range(CHIPS)][1:]
    random.Random(4).shuffle(offsets)
    offsets.sort(key=lambda o: -sum(min(d, CHIPS - d) for d in o))
    return offsets


def block(ref, side, k=None):
    def column(c):
        part = ref[side, :, c] if k is None else ref[side, :, c, k]
        return part.reshape(128, 128)

    return [jnp.concatenate([column(2 * j), column(2 * j + 1)], axis=1) for j in range(4)]


def labels(mine, theirs):
    return jnp.where(mine == theirs, 1.0, -1.0).astype(jnp.float32)


def slope(mine, theirs, label, sharpness, shift):
    score = jnp.zeros((128, 128), jnp.float32)
    for p, q in zip(mine, theirs):
        score += lax.dot_general(p, q, (((1,), (1,)), ((), ())), preferred_element_type=jnp.float32)
    logit = sharpness * score + shift
    return (-sharpness * label * jax.nn.sigmoid(-label * logit)).astype(jnp.bfloat16)


def far_product(mine, theirs, label, sharpness, shift):
    g = jnp.concatenate(
        [slope(mine, t, label[k], sharpness, shift) for k, t in enumerate(theirs)], axis=1
    )
    for j in range(4):
        slab = jnp.concatenate([t[j] for t in theirs], axis=0)
        yield pl.ds(j * 256, 256), jnp.dot(g, slab, preferred_element_type=jnp.float32)


def kernel(
    a_ref,
    b_ref,
    ida_ref,
    idb_ref,
    opponent_hbm,
    sharpness_ref,
    offset_ref,
    grad_a_ref,
    grad_b_ref,
    own,
    far,
    label_ref,
    raw,
    ids,
    opponent_ref,
    mid,
    out,
    load_sem,
    send_sem,
    recv_sem,
):
    rounds = opponent_ref.shape[0]
    loads = [
        pltpu.make_async_copy(src, dst, load_sem.at[i])
        for i, (src, dst) in enumerate(
            (
                (a_ref, raw.at[0]),
                (b_ref, raw.at[1]),
                (ida_ref, ids.at[0]),
                (idb_ref, ids.at[1]),
                (opponent_hbm, opponent_ref),
            )
        )
    ]
    for load in loads:
        load.start()

    row, col = lax.axis_index("row"), lax.axis_index("col")
    x, z_lo = row % CHIPS, row // CHIPS
    y, z_hi, core = col // CHIPS, (col // 2) % 2, col % 2
    z = z_hi * 2 + z_lo
    me = row * 16 + col

    xs = [(x + d) % CHIPS for d in range(CHIPS)]
    ys = [(y + d) % CHIPS for d in range(CHIPS)]
    zs = [(z + d) % CHIPS for d in range(CHIPS)]
    index_x = [v * 16 for v in xs]
    index_y = [v * 4 for v in ys]
    index_z = [(v % 2) * 64 + (v // 2) * 2 for v in zs]
    group_x = [v // 2 for v in xs]
    group_z = [v * 2 for v in zs]
    column_x = [(v % 2) * 4 for v in xs]

    def device(o):
        return index_x[o[0]] + index_y[o[1]] + index_z[o[2]] + o[3]

    def tile_of(o):
        return o[3], group_z[o[2]] + group_x[o[0]], column_x[o[0]] + ys[o[1]]

    chips = far_first()
    here, beside = (0, 0, 0, core), (0, 0, 0, 1 - core)
    spread = [beside] + [o + (c,) for c in range(2) for o in chips]
    deliver = [o + (c,) for _, c, o in sorted([(i + 36 * (c != 1), c, o) for i, o in enumerate(chips) for c in range(2)])] + [beside]
    barrier = pltpu.get_barrier_semaphore()
    for o in [o + (c,) for o in chips for c in range(2)] + [beside]:
        pl.semaphore_signal(barrier, inc=1, device_id=device(o), device_id_type=LOGICAL)

    for side in range(2):
        loads[side].wait()
        for g in range(8):
            value = raw[side, pl.ds(g * 16, 16), :]
            scale = lax.rsqrt(jnp.sum(value * value, axis=-1, keepdims=True) + 1e-06)
            value = (value * scale).astype(jnp.bfloat16)
            for c in range(8):
                own[side, g, c] = value[:, c * 128 : (c + 1) * 128]

    pl.semaphore_wait(barrier, len(deliver))

    for o in spread:
        pltpu.make_async_remote_copy(
            src_ref=own.at[tile_of(o)],
            dst_ref=mid.at[me],
            send_sem=send_sem.at[0],
            recv_sem=recv_sem.at[0],
            device_id=device(o),
            device_id_type=LOGICAL,
        ).start()
    my_tile = tile_of(here)
    pltpu.make_async_copy(own.at[my_tile], mid.at[me], recv_sem.at[0]).start()

    sharpness = sharpness_ref[0]
    shift = offset_ref[0]

    for load in loads[2:]:
        load.wait()
    grads = (grad_a_ref, grad_b_ref)
    my_ids = []
    for side in range(2):
        line = ids[side, pl.ds(me, 1), :]
        my_ids.append(jnp.transpose(jnp.broadcast_to(line, (128, 128))))
    for side in range(2):
        theirs = block(own, 1 - side)
        label = labels(my_ids[side], ids[1 - side, pl.ds(me, 1), :])
        g = slope(block(own, side), theirs, label, sharpness, shift)
        for j in range(4):
            grads[side][:, j * 256 : (j + 1) * 256] = jnp.dot(g, theirs[j], preferred_element_type=jnp.float32)

    far_label = [
        [labels(my_ids[side], ids[1 - side, pl.ds(opponent_ref[k, me], 1), :]) for k in range(rounds)]
        for side in range(2)
    ]
    for k in range(rounds):
        label_ref[k] = far_label[0][k]

    pltpu.make_async_copy(mid, mid, recv_sem.at[0]).wait()

    def fetch(there):
        for k in range(rounds):
            out[there, k] = mid[opponent_ref[k, there]]

    for o in deliver:
        there = device(o)
        fetch(there)
        pltpu.make_async_remote_copy(
            src_ref=out.at[there],
            dst_ref=far.at[my_tile],
            send_sem=send_sem.at[1],
            recv_sem=recv_sem.at[1 + core],
            device_id=there,
            device_id_type=LOGICAL,
        ).start()
    fetch(me)
    pltpu.make_async_copy(out.at[me], far.at[my_tile], recv_sem.at[1 + core]).start()

    pltpu.make_async_copy(far.at[0], far.at[0], recv_sem.at[1]).wait()
    theirs = [block(far, 0, k) for k in range(rounds)]
    for columns, product in far_product(block(own, 1), theirs, far_label[1], sharpness, shift):
        grad_b_ref[:, columns] += product
    pltpu.make_async_copy(far.at[1], far.at[1], recv_sem.at[2]).wait()

    spread_out = mid.at[pl.ds(0, len(spread))]
    pltpu.make_async_copy(spread_out, spread_out, send_sem.at[0]).wait()
    sent = out.at[pl.ds(0, len(deliver))]
    pltpu.make_async_copy(sent, sent, send_sem.at[1]).wait()


def finish(sharpness_ref, offset_ref, part_a, grad_b, own, far, label_ref, out_a, out_b, total, sem):
    copies = [pltpu.make_async_copy(grad_b, out_b, sem.at[4])]
    copies[0].start()
    rounds = label_ref.shape[0]
    theirs = [block(far, 1, k) for k in range(rounds)]
    label = [label_ref[k] for k in range(rounds)]
    for j, (columns, product) in enumerate(
        far_product(block(own, 0), theirs, label, sharpness_ref[0], offset_ref[0])
    ):
        total[:, columns] = part_a[:, columns] + product
        copies.append(pltpu.make_async_copy(total.at[:, columns], out_a.at[:, columns], sem.at[j]))
        copies[-1].start()
    for copy in copies:
        copy.wait()


def shards(
    anchor_features,
    candidate_features,
    anchor_sample_ids,
    candidate_sample_ids,
    opponent_tile,
    sharpness_array,
    score_offset,
):
    rows, width = anchor_features.shape
    rounds, blocks = opponent_tile.shape
    hbm = pl.BlockSpec(memory_space=pltpu.HBM)
    vmem = pl.BlockSpec(memory_space=pltpu.VMEM)
    smem = pl.BlockSpec(memory_space=pltpu.SMEM)
    grad = jax.ShapeDtypeStruct((rows, width), jnp.float32)
    parts = pl.pallas_call(
        kernel,
        out_shape=(
            grad,
            grad,
            jax.ShapeDtypeStruct((2, 8, 8) + TILE, jnp.bfloat16),
            jax.ShapeDtypeStruct((2, 8, 8, rounds) + TILE, jnp.bfloat16),
            jax.ShapeDtypeStruct((rounds, rows, rows), jnp.float32),
        ),
        in_specs=[hbm, hbm, hbm, hbm, hbm, smem, smem],
        out_specs=(vmem,) * 5,
        scratch_shapes=[
            pltpu.VMEM((2, rows, width), jnp.float32),
            pltpu.VMEM((2, blocks, rows), jnp.int32),
            pltpu.SMEM((rounds, blocks), jnp.int32),
            pltpu.VMEM((blocks,) + TILE, jnp.bfloat16),
            pltpu.VMEM((blocks, rounds) + TILE, jnp.bfloat16),
            pltpu.SemaphoreType.DMA((5,)),
            pltpu.SemaphoreType.DMA((2,)),
            pltpu.SemaphoreType.DMA((3,)),
        ],
        compiler_params=pltpu.CompilerParams(
            collective_id=0, has_side_effects=True, vmem_limit_bytes=32 * 1024 * 1024
        ),
        name="spread_deliver",
    )(
        in_hbm(anchor_features),
        in_hbm(candidate_features),
        in_hbm(anchor_sample_ids.reshape(blocks, rows)),
        in_hbm(candidate_sample_ids.reshape(blocks, rows)),
        in_hbm(opponent_tile),
        sharpness_array,
        score_offset,
    )
    return pl.pallas_call(
        finish,
        out_shape=(grad, grad),
        in_specs=[smem, smem] + [vmem] * 5,
        out_specs=(hbm, hbm),
        scratch_shapes=[pltpu.VMEM((rows, width), jnp.float32), pltpu.SemaphoreType.DMA((5,))],
        compiler_params=pltpu.CompilerParams(vmem_limit_bytes=16 * 1024 * 1024),
        name="finish",
    )(sharpness_array, score_offset, *[in_vmem(p) for p in parts])


def solution(mesh):
    placed = (P(("row", "col"), None), P(("row", "col"), None), P(), P(), P(), P(), P())
    return jax.shard_map(
        shards,
        mesh=mesh,
        in_specs=placed,
        out_specs=(P(("row", "col"), None), P(("row", "col"), None)),
        check_vma=False,
    )
```
